256 devices in a mesh: dp: 16 (over z, core), expert: 16 (over y, x).
Axes of the slice: x: 4, y: 4, z: 8, core: 2. Of those that a mesh axis runs over, the one named last changes fastest.
Arguments:
- dy_tokens: bfloat16 [131072, 4096], P(('dp', 'expert')), may hold values from -6 to 6
- gates: bfloat16 [131072, 8], P(('dp', 'expert')), may hold values from 0.049804688 to 1
- routes: int32 [131072, 8], P(('dp', 'expert')), may hold values from 0 to 127, as said below
- hidden: bfloat16 [16, 16384, 1536], P('expert', 'dp'), may hold values from -6 to 6
- projector: bfloat16 [16, 1536, 256], P('expert'), may hold values from -0.15625 to 0.15625
- weights: bfloat16 [16, 1536, 4096], P('expert', None, 'dp'), may hold values from -0.15625 to 0.15625
- moment_one: float32 [4096, 16, 256], P('dp', 'expert'), may hold values from -6 to 6
- moment_two: float32 [4096, 16, 256], P('dp', 'expert'), may hold values from 0.25 to 4
Outputs:
- new_weights: bfloat16 [16, 1536, 4096], P('expert', None, 'dp')
- new_moment_one: float32 [4096, 16, 256], P('dp', 'expert')
- new_moment_two: float32 [4096, 16, 256], P('dp', 'expert')
The draws below stay inside these ranges and needn't reach their ends.
Inputs may be any that keep to these rules, and one draw needn't show every extreme that they name: `routes`: each row names 8 different experts, one from each group of 16 consecutive ids, so exactly one below 16; among the 512 rows of one device no expert below 16 is named more than 64 times, and some such expert exactly 64 times.
All inputs are finite; a program needn't handle non-finite values.
Results may differ from the reference program's by a relative error of at most 0.0035.
Values may be sent and summed in bfloat16 or wider, within the bound.
A program may use at most 192 MiB of HBM per device.

```python
import math
import jax
import jax.numpy as jnp
from jax import lax

D = 4096
FF = 1536
RANK = 256
EXPERTS = 16
TOP = 8
TOK_DEV = 512
CAP = 64
TOKENS = 131072
SLOTS = 16384


def draw_routes(key, part):
    key = jax.random.fold_in(key, 11)
    blocks = TOKENS // TOK_DEV
    key_hot, key_perm, key_band, key_col, key_len, key_others = jax.random.split(key, 6)
    hot = jax.random.randint(key_hot, (blocks,), 0, EXPERTS)
    cycle = jax.random.randint(key_len, (blocks,), 8, EXPERTS)
    other_scores = jax.random.randint(key_others, (blocks, EXPERTS - 1), 0, 2 ** 20) * (EXPERTS - 1) + jnp.arange(EXPERTS - 1)[None, :]
    other_order = jnp.argsort(other_scores, axis=1).astype(jnp.int32)
    position = jnp.arange(TOK_DEV, dtype=jnp.int32)
    which = (position[None, :] - CAP) % cycle[:, None]
    picked_other = jnp.take_along_axis(other_order, which, axis=1)
    other = (hot[:, None] + 1 + picked_other) % EXPERTS
    label = jnp.where(position[None, :] < CAP, hot[:, None], other)
    token_scores = jax.random.randint(key_perm, (blocks, TOK_DEV), 0, 2 ** 20) * TOK_DEV + position[None, :]
    token_order = jnp.argsort(token_scores, axis=1).astype(jnp.int32)
    window = jnp.take_along_axis(label, token_order, axis=1)
    band_ids = jax.random.randint(key_band, (blocks, TOK_DEV, TOP - 1), 0, EXPERTS)
    band_base = (jnp.arange(TOP - 1, dtype=jnp.int32) + 1) * EXPERTS
    full = jnp.concatenate([window[:, :, None], band_ids + band_base[None, None, :]], axis=2)
    col_scores = jax.random.randint(key_col, (blocks, TOK_DEV, TOP), 0, 2 ** 20) * TOP + jnp.arange(TOP, dtype=jnp.int32)[None, None, :]
    col_order = jnp.argsort(col_scores, axis=2).astype(jnp.int32)
    full = jnp.take_along_axis(full, col_order, axis=2)
    return full.reshape(TOKENS, TOP).astype(jnp.int32)


def shard_levels(key, dims, cuts, low, largest):
    gain, own = 1.0, jax.random.fold_in(key, 6)
    for axis_at, parts in cuts:
        steps = jnp.exp(jax.random.uniform(jax.random.fold_in(own, axis_at), (parts,), jnp.float32, low / len(cuts), largest / len(cuts)))
        gain = gain * jnp.repeat(steps, dims[axis_at] // parts).reshape([-1 if axis == axis_at else 1 for axis in range(len(dims))])
    return gain


def noise(stream_key, shape, spread, limit, shards=(), kind=jnp.bfloat16):
    level = shard_levels(stream_key, shape, shards, -0.22, 0.18) if shards else 1.0
    entries = jax.random.normal(stream_key, shape, jnp.float32) * spread * level
    return jnp.minimum(jnp.maximum(entries, -limit), limit).astype(kind)


def setup_inputs(seed: int = 0) -> dict:
    key_of = jax.random.split(jax.random.key(seed), 9)
    dy_tokens = noise(key_of[0], (TOKENS, D), 1.0, 6.0, ((0, 256),))
    gates = jnp.clip(jnp.exp(math.log(1.0) - 2.9996462 * jax.random.uniform(key_of[1], (TOKENS, TOP), jnp.float32) ** shard_levels(key_of[1], (TOKENS, TOP), ((0, 256),), -0.2, 0.2)), 0.049804688, 1.0).astype(jnp.bfloat16)
    routes = draw_routes(jax.random.fold_in(key_of[8], 71), 0)
    hidden = noise(key_of[3], (EXPERTS, SLOTS, FF), 1.0, 6.0, ((0, 16), (1, 16)))
    projector = noise(key_of[4], (EXPERTS, FF, RANK), FF ** -0.5, 0.15625, ((0, 16),))
    weights = noise(key_of[5], (EXPERTS, FF, D), FF ** -0.5, 0.15625, ((0, 16), (2, 16)))
    moment_one = noise(key_of[6], (D, EXPERTS, RANK), 1.0, 6.0, ((0, 16), (1, 16)), jnp.float32)
    moment_two = jnp.clip(jnp.exp(math.log(4.0) - 2.7725887 * jax.random.uniform(key_of[7], (D, EXPERTS, RANK), jnp.float32) ** shard_levels(key_of[7], (D, EXPERTS, RANK), ((0, 16), (1, 16)), -0.2, 0.2)), 0.25, 4.0)
    return {"dy_tokens": dy_tokens, "gates": gates, "routes": routes, "hidden": hidden, "projector": projector, "weights": weights, "moment_one": moment_one, "moment_two": moment_two}


grad_scale = 1.0
beta_one = 0.9
beta_two = 0.999
eps = 1e-06
step_size = 0.02

def reference(dy_tokens, gates, routes, hidden, projector, weights, moment_one, moment_two):
    tokens = dy_tokens.shape[0]
    blocks = tokens // TOK_DEV
    labels = jnp.arange(EXPERTS, dtype=jnp.int32)
    onehot = routes[:, :, None] == labels[None, None, :]
    member = lax.optimization_barrier(jnp.sum(onehot.astype(jnp.int32), axis=1))
    rank = jnp.cumsum(member.reshape(blocks, TOK_DEV, EXPERTS), axis=1).reshape(tokens, EXPERTS) - 1
    source = jnp.arange(tokens, dtype=jnp.int32) // TOK_DEV
    slot_index = source[:, None] * CAP + rank
    weight = lax.optimization_barrier(jnp.sum(jnp.where(onehot, gates.astype(jnp.float32)[:, :, None], 0.0), axis=1))

    def one_expert(expert):
        proj = projector[expert]
        reduced = jnp.dot(hidden[expert], proj, preferred_element_type=jnp.float32).astype(jnp.bfloat16)
        chosen = member[:, expert] > 0
        rows = jnp.where(chosen, slot_index[:, expert], 0).astype(jnp.int32)
        picked = jnp.where(chosen[:, None], reduced[rows].astype(jnp.float32), 0.0)
        scaled = (dy_tokens.astype(jnp.float32) * weight[:, expert][:, None]).astype(jnp.bfloat16)
        scaled = lax.optimization_barrier(scaled).astype(jnp.float32)
        return jnp.dot(scaled.T, picked, precision=lax.Precision.HIGHEST) * grad_scale
    grads = lax.map(one_expert, labels)
    grad = jnp.transpose(grads, (1, 0, 2))
    new_one = beta_one * moment_one + (1.0 - beta_one) * grad
    new_two = beta_two * moment_two + (1.0 - beta_two) * grad * grad
    direction = (new_one / (jnp.sqrt(new_two) + eps)).astype(jnp.bfloat16)
    update = jnp.einsum('efr,der->efd', projector.astype(jnp.float32), direction.astype(jnp.float32), precision=lax.Precision.HIGHEST)
    new_weights = (weights.astype(jnp.float32) - step_size * update).astype(jnp.bfloat16)
    return (new_weights, new_one, new_two)
```

```python
import jax
import jax.numpy as jnp
from jax import lax
from jax.experimental import pallas as pl
from jax.experimental.pallas import tpu as pltpu
from jax.sharding import PartitionSpec as P

EXPERTS = 16
CAP = 64
GX, GY, GZ = 4, 4, 8
MESH = pl.DeviceIdType.MESH

beta_one = 0.9
beta_two = 0.999
eps = 1e-06
step_size = 0.02

F32, BF16 = jnp.float32, jnp.bfloat16


def dot(a, b):
    return jnp.dot(a, b, preferred_element_type=F32)


def dot_nt(a, b):
    return lax.dot_general(a, b, (((1,), (1,)), ((), ())), preferred_element_type=F32)


def eye(n):
    same = lax.broadcasted_iota(jnp.int32, (n, n), 0) == lax.broadcasted_iota(jnp.int32, (n, n), 1)
    return jnp.where(same, 1.0, 0.0).astype(BF16)


def grad_kernel(
    dy, routes, gates, hidden, projector, grad,
    dyb, hid, proj, pmat, pk, rl, ra, rt, rx, zs, zr, fs, fr,
    load_sem, dy_sem, r_send, r_recv, pk_send, rx_recv, z_send, z_recv, f_send, f_recv,
):
    dp, ex = lax.axis_index("dp"), lax.axis_index("expert")
    x, y, z, c = ex % GX, ex // GX, dp // 2, dp % 2

    def dev(x, y, z, c):
        return (z * 2 + c, y * GX + x)

    def remote(src, dst, send, recv, to):
        return pltpu.make_async_remote_copy(src, dst, send, recv, device_id=to, device_id_type=MESH)

    row = [(dx, 0, dc) for dx in range(GX) for dc in range(2)]
    col = [(0, ddy, dc) for ddy in range(GY) for dc in range(2)]

    def far(s):
        return (8 - s) // 2

    def slab(s):
        return (z + jnp.where(s % 2 == 0, far(s), GZ - far(s))) % GZ

    def load_dy(s):
        width = dyb.shape[2]
        return pltpu.make_async_copy(
            dy.at[:, pl.ds(pl.multiple_of(slab(s) * width, width), width)], dyb.at[s], dy_sem.at[s]
        )

    load_hid = pltpu.make_async_copy(hidden, hid, load_sem.at[0])
    load_proj = pltpu.make_async_copy(projector, proj, load_sem.at[1])
    load_proj.start()
    load_hid.start()

    @pl.loop(0, GZ)
    def _(s):
        load_dy(s).start()

    barrier = pltpu.get_barrier_semaphore()
    partners = [dev((x + a) % GX, (y + b) % GY, z, (c + d) % 2) for a, b, d in row[1:] + col[2:]]
    partners += [dev(x, y, (z + 1) % GZ, c), dev(x, y, (z + GZ - 1) % GZ, c)]
    for to in partners:
        pl.semaphore_signal(barrier, inc=1, device_id=to, device_id_type=MESH)

    zr[0, 3, 1] = jnp.zeros(zr.shape[3:], BF16)
    zr[1, 3, 0] = jnp.zeros(zr.shape[3:], BF16)

    tokens = routes.shape[1]
    ids = routes[...]
    here = ids < EXPERTS
    expert = jnp.sum(jnp.where(here, ids, 0), axis=0, keepdims=True)
    gate = jnp.sum(jnp.where(here, gates[...].astype(F32), 0.0), axis=0, keepdims=True)
    chosen = lax.broadcasted_iota(jnp.int32, (EXPERTS, tokens), 0) == expert
    earlier = lax.broadcasted_iota(jnp.int32, (tokens, tokens), 0) < lax.broadcasted_iota(
        jnp.int32, (tokens, tokens), 1
    )
    count = dot(jnp.where(chosen, 1.0, 0.0).astype(BF16), jnp.where(earlier, 1.0, 0.0).astype(BF16))
    rank = jnp.sum(jnp.where(chosen, count, 0.0), axis=0, keepdims=True).astype(jnp.int32)
    slot = expert * CAP + rank
    for e in range(0, EXPERTS, 4):
        at = lax.broadcasted_iota(jnp.int32, (4 * CAP, tokens), 0) + e * CAP
        pmat[e * CAP : (e + 4) * CAP, :] = jnp.where(at == slot, gate, 0.0).astype(BF16)

    load_proj.wait()
    load_hid.wait()
    for b in range(GY):
        rows = GX * CAP
        part = dot(hid[b * rows : (b + 1) * rows, :], proj[...]).astype(BF16)
        rl[b] = part.reshape(GX, CAP, part.shape[1])

    pl.semaphore_wait(barrier, len(partners))

    def reduced_copy(h, k):
        if h == 0:
            to = (y + k) % GY
            return rl.at[to], ra.at[0, y % 2, c], r_send.at[h, k], r_recv.at[h, y % 2, c], dev(x, to, z, y // 2)
        to = (x + k) % GX
        return rl.at[:, to], ra.at[1, x % 2, c], r_send.at[h, k], r_recv.at[h, x % 2, c], dev(to, y, z, x // 2)

    stays = [y // 2 == c, x // 2 == c]
    for k in range(4):
        for h in range(2):
            src, dst, ss, rs, to = reduced_copy(h, k)
            if k:
                remote(src, dst, ss, rs, to).start()
            else:
                pl.when(stays[h])(lambda: pltpu.make_async_copy(src, dst, rs).start())
                pl.when(jnp.logical_not(stays[h]))(lambda: remote(src, dst, ss, rs, to).start())

    def row_copy(s, h, n):
        if h == 0:
            dx, _, dc = row[n]
            tx, tc = (x + dx) % GX, (c + dc) % 2
            return pk.at[s, 0, pl.ds(2 * tc, 2), tx], rx.at[s, 0, :, c, x], dev(tx, y, z, tc)
        _, ddy, dc = col[n]
        ty, tc = (y + ddy) % GY, (c + dc) % 2
        return pk.at[s, 1, ty, pl.ds(2 * tc, 2)], rx.at[s, 1, :, c, y], dev(x, ty, z, tc)

    @pl.loop(0, GZ)
    def _(s):
        load_dy(s).wait()
        packed = dot(pmat[...], dyb[s]).astype(BF16)
        half = packed.shape[1] // 2
        for h in range(2):
            pk[s, h] = packed[:, h * half : (h + 1) * half].reshape(GY, GX, CAP, half)
        for n in range(8):
            for h in range(2):
                src, dst, to = row_copy(s, h, n)
                if n:
                    remote(src, dst, pk_send.at[s, h, n], rx_recv.at[s, h], to).start()
                else:
                    pltpu.make_async_copy(src, dst, rx_recv.at[s, h]).start()

    def landed(buf, sem):
        pltpu.make_async_copy(buf, buf, sem).wait()

    for h in range(2):
        for e in range(2):
            for k in range(2):
                landed(ra.at[h, e, k], r_recv.at[h, e, k])
            got = ra[h, e].reshape(8 * CAP, ra.shape[-1])
            rt[h, e] = dot_nt(eye(got.shape[1]), got).astype(BF16)

    def partial(s, h, e):
        got = rx[s, h, e]
        return dot(rt[h, e], got.reshape(8 * CAP, got.shape[-1]))

    def z_copy(s, h, e, way, k):
        to = dev(x, y, (z + jnp.where(way == 0, 1, GZ - 1)) % GZ, c)
        return remote(
            zs.at[s, h, e], zr.at[way, k - 1, h, e], z_send.at[s, h, e], z_recv.at[way, k - 1, h, e], to
        )

    for h in range(2):
        landed(rx.at[0, h], rx_recv.at[0, h])
        for e in range(2):
            zs[0, h, e] = partial(0, h, e).astype(BF16)
            z_copy(0, h, e, h, 4).start()

    @pl.loop(1, 7)
    def _(s):
        way, k = s % 2, far(s)
        for h in range(2):
            landed(rx.at[s, h], rx_recv.at[s, h])
            for e in range(2):
                total = partial(s, h, e)

                @pl.when(s != h + 1)
                def _():
                    landed(zr.at[way, k, h, e], z_recv.at[way, k, h, e])

                zs[s, h, e] = (total + zr[way, k, h, e].astype(F32)).astype(BF16)
                z_copy(s, h, e, way, k).start()

    def owner_copy(h, e):
        to = 2 * c + e
        if h == 0:
            return fs.at[0, e], fr.at[y], f_send.at[h, e], f_recv.at[y], dev(x, to, z, 0), (to == y) & (c == 0)
        return fs.at[1, e], fr.at[x], f_send.at[h, e], f_recv.at[x], dev(to, y, z, 1), (to == x) & (c == 1)

    for h in range(2):
        landed(rx.at[7, h], rx_recv.at[7, h])
        for e in range(2):
            total = partial(7, h, e)
            for way in range(2):
                landed(zr.at[way, 0, h, e], z_recv.at[way, 0, h, e])
                total = total + zr[way, 0, h, e].astype(F32)
            fs[h, e] = total.astype(BF16)
            src, dst, ss, rs, to, own = owner_copy(h, e)
            pl.when(own)(lambda: pltpu.make_async_copy(src, dst, rs).start())
            pl.when(jnp.logical_not(own))(lambda: remote(src, dst, ss, rs, to).start())

    for k in range(4):
        landed(fr.at[k], f_recv.at[k])
    total = fr[0].astype(F32)
    for k in range(1, 4):
        total = total + fr[k].astype(F32)
    grad[...] = total.T

    for h in range(2):
        for k in range(4):
            src, dst, ss, rs, to = reduced_copy(h, k)
            if k:
                remote(src, dst, ss, rs, to).wait_send()
            else:
                pl.when(jnp.logical_not(stays[h]))(lambda: remote(src, dst, ss, rs, to).wait_send())
        for e in range(2):
            src, dst, ss, rs, to, own = owner_copy(h, e)
            pl.when(jnp.logical_not(own))(lambda: remote(src, dst, ss, rs, to).wait_send())

    @pl.loop(0, GZ)
    def _(s):
        for h in range(2):
            for n in range(1, 8):
                src, dst, to = row_copy(s, h, n)
                remote(src, dst, pk_send.at[s, h, n], rx_recv.at[s, h], to).wait_send()

    @pl.loop(0, 7)
    def _(s):
        for h in range(2):
            for e in range(2):
                z_copy(s, h, e, 0, 1).wait_send()


def grads(dy, routes, gates, hidden, projector):
    tokens, width = dy.shape
    slots, features = hidden.shape
    rank = projector.shape[1]
    slab = width // GZ
    half = slab // 2
    dma = pltpu.SemaphoreType.DMA
    return pl.pallas_call(
        grad_kernel,
        out_shape=jax.ShapeDtypeStruct((half, rank), F32),
        in_specs=[
            pl.BlockSpec(memory_space=pl.ANY),
            pl.BlockSpec(memory_space=pltpu.VMEM),
            pl.BlockSpec(memory_space=pltpu.VMEM),
            pl.BlockSpec(memory_space=pl.ANY),
            pl.BlockSpec(memory_space=pl.ANY),
        ],
        out_specs=pl.BlockSpec(memory_space=pltpu.VMEM),
        scratch_shapes=[
            pltpu.VMEM((GZ, tokens, slab), BF16),
            pltpu.VMEM((slots, features), BF16),
            pltpu.VMEM((features, rank), BF16),
            pltpu.VMEM((EXPERTS * CAP, tokens), BF16),
            pltpu.VMEM((GZ, 2, GY, GX, CAP, half), BF16),
            pltpu.VMEM((GY, GX, CAP, rank), BF16),
            pltpu.VMEM((2, 2, 2, 4, CAP, rank), BF16),
            pltpu.VMEM((2, 2, rank, 8 * CAP), BF16),
            pltpu.VMEM((GZ, 2, 2, 2, 4, CAP, half), BF16),
            pltpu.VMEM((7, 2, 2, rank, half), BF16),
            pltpu.VMEM((2, 4, 2, 2, rank, half), BF16),
            pltpu.VMEM((2, 2, rank, half), BF16),
            pltpu.VMEM((4, rank, half), BF16),
            dma((2,)),
            dma((GZ,)),
            dma((2, 4)),
            dma((2, 2, 2)),
            dma((GZ, 2, 8)),
            dma((GZ, 2)),
            dma((7, 2, 2)),
            dma((2, 4, 2, 2)),
            dma((2, 2)),
            dma((4,)),
        ],
        compiler_params=pltpu.CompilerParams(
            collective_id=0, has_side_effects=True, vmem_limit_bytes=58 * 2**20
        ),
        cost_estimate=pl.CostEstimate(flops=8 * 10**9, bytes_accessed=8 * 2**20, transcendentals=0),
    )(dy, routes, gates, hidden, projector)


def update_kernel(grad, one, two, projector, weights, new_weights, new_one, new_two):
    g = grad[...]
    first = beta_one * one[:, 0, :] + (1.0 - beta_one) * g
    second = beta_two * two[:, 0, :] + (1.0 - beta_two) * g * g
    new_one[:, 0, :] = first
    new_two[:, 0, :] = second
    direction = (first / (jnp.sqrt(second) + eps)).astype(BF16)
    for at in range(0, weights.shape[0], 256):
        rows = slice(at, at + 256)
        change = dot_nt(projector[rows, :], direction)
        new_weights[rows, :] = (weights[rows, :].astype(F32) - step_size * change).astype(BF16)


def update(grad, one, two, projector, weights):
    return pl.pallas_call(
        update_kernel,
        out_shape=(
            jax.ShapeDtypeStruct(weights.shape, BF16),
            jax.ShapeDtypeStruct(one.shape, F32),
            jax.ShapeDtypeStruct(two.shape, F32),
        ),
        compiler_params=pltpu.CompilerParams(vmem_limit_bytes=32 * 2**20),
    )(grad, one, two, projector, weights)


def body(dy_tokens, gates, routes, hidden, projector, weights, moment_one, moment_two):
    projector = projector[0]
    grad = grads(dy_tokens, routes.T, gates.T, hidden[0], projector)
    new_weights, new_one, new_two = update(grad, moment_one, moment_two, projector, weights[0])
    return (new_weights[None], new_one, new_two)


def solution(mesh):
    in_specs = (
        P(("dp", "expert"), None),
        P(("dp", "expert"), None),
        P(("dp", "expert"), None),
        P("expert", "dp", None),
        P("expert", None, None),
        P("expert", None, "dp"),
        P("dp", "expert", None),
        P("dp", "expert", None),
    )
    out_specs = (P("expert", None, "dp"), P("dp", "expert", None), P("dp", "expert", None))
    return jax.shard_map(body, mesh=mesh, in_specs=in_specs, out_specs=out_specs, check_vma=False)
```

```python
import jax
import jax.numpy as jnp
from jax import lax
from jax.experimental import pallas as pl
from jax.experimental.pallas import tpu as pltpu
from jax.sharding import PartitionSpec as P

EXPERTS = 16
CAP = 64
GX, GY, GZ = 4, 4, 8
LEAD = 3
PIECES = 2
MESH = pl.DeviceIdType.MESH

beta_one = 0.9
beta_two = 0.999
eps = 1e-06
step_size = 0.02

F32, BF16 = jnp.float32, jnp.bfloat16


def dot(a, b):
    return jnp.dot(a, b, preferred_element_type=F32)


def dot_nt(a, b):
    return lax.dot_general(a, b, (((1,), (1,)), ((), ())), preferred_element_type=F32)


def eye(n):
    same = lax.broadcasted_iota(jnp.int32, (n, n), 0) == lax.broadcasted_iota(jnp.int32, (n, n), 1)
    return jnp.where(same, 1.0, 0.0).astype(BF16)


SPOTS = ((0, 0), (1, 1), (3, 2), (2, 3))
TAKES = (
    ((0, 0), (0, 1), (0, 3), (3, 0)),
    ((1, 1), (1, 0), (1, 2), (2, 1)),
    ((3, 2), (0, 2), (2, 2), (3, 1)),
    ((2, 3), (1, 3), (2, 0), (3, 3)),
)


def grad_kernel(
    dy, routes, gates, hidden, projector, grad,
    dyb, hid, proj, pmat, pk, rl, ra, rt, rx, zs, zr, fs, fr,
    load_sem, dy_sem, r_send, r_recv, pk_send, rx_recv, z_send, z_recv, f_send, f_recv,
):
    dp, ex = lax.axis_index("dp"), lax.axis_index("expert")
    x, y, z, c = ex % GX, ex // GX, dp // 2, dp % 2

    def dev(x, y, z, c):
        return (z * 2 + c, y * GX + x)

    def near(dx, dy, c):
        return dev((x + dx) % GX, (y + dy) % GY, z, c)

    def remote(src, dst, send, recv, to):
        return pltpu.make_async_remote_copy(src, dst, send, recv, device_id=to, device_id_type=MESH)

    def landed(buf, sem):
        pltpu.make_async_copy(buf, buf, sem).wait()

    def far(s):
        return (8 - s) // 2

    def way_of(s, h):
        return (s + h) % 2

    def load_dy(s, h):
        half = dyb.shape[2] // 2
        slab = (z + jnp.where(way_of(s, h) == 0, far(s), GZ - far(s))) % GZ
        at = pl.multiple_of((slab * 2 + h) * half, half)
        return pltpu.make_async_copy(
            dy.at[:, pl.ds(at, half)], dyb.at[s, :, pl.ds(h * half, half)], dy_sem.at[s, h]
        )

    def load_hid(spot, j):
        dx, ddy = TAKES[spot][j]
        block = (y + ddy) % GY * GX + (x + dx) % GX
        return pltpu.make_async_copy(
            hidden.at[pl.ds(pl.multiple_of(block * CAP, CAP), CAP)], hid.at[spot, pl.ds(j * CAP, CAP)], load_sem.at[spot, j]
        )

    load_proj = pltpu.make_async_copy(projector, proj, load_sem.at[4, 0])
    for h in range(2):
        load_dy(0, h).start()
    load_proj.start()
    for spot in (0, 2, 1, 3):
        for j in range(4):
            load_hid(spot, j).start()

    @pl.loop(1, GZ)
    def _(s):
        for h in range(2):
            load_dy(s, h).start()

    barrier = pltpu.get_barrier_semaphore()
    steps = [(1, 0), (3, 0), (0, 1), (0, 3)]
    for dx, ddy in SPOTS[1:]:
        steps += [(dx, ddy), ((GX - dx) % GX, (GY - ddy) % GY)]
    partners = [near(dx, ddy, core) for dx, ddy in steps for core in range(2)] + [dev(x, y, z, 1 - c)]
    partners += [dev(x, y, (z + 1) % GZ, c), dev(x, y, (z + GZ - 1) % GZ, c)]
    for to in partners:
        pl.semaphore_signal(barrier, inc=1, device_id=to, device_id_type=MESH)

    zr[0, 3, 1] = jnp.zeros(zr.shape[3:], BF16)
    zr[1, 3, 0] = jnp.zeros(zr.shape[3:], BF16)

    tokens = routes.shape[1]
    ids = routes[...]
    here = ids < EXPERTS
    expert = jnp.sum(jnp.where(here, ids, 0), axis=0, keepdims=True)
    gate = jnp.sum(jnp.where(here, gates[...].astype(F32), 0.0), axis=0, keepdims=True)
    chosen = lax.broadcasted_iota(jnp.int32, (EXPERTS, tokens), 0) == expert
    earlier = lax.broadcasted_iota(jnp.int32, (tokens, tokens), 0) < lax.broadcasted_iota(
        jnp.int32, (tokens, tokens), 1
    )
    count = dot(jnp.where(chosen, 1.0, 0.0).astype(BF16), jnp.where(earlier, 1.0, 0.0).astype(BF16))
    rank = jnp.sum(jnp.where(chosen, count, 0.0), axis=0, keepdims=True).astype(jnp.int32)
    slot = expert * CAP + rank
    for e in range(0, EXPERTS, 4):
        at = lax.broadcasted_iota(jnp.int32, (4 * CAP, tokens), 0) + e * CAP
        pmat[e * CAP : (e + 4) * CAP, :] = jnp.where(at == slot, gate, 0.0).astype(BF16)

    def pack(s):
        for h in range(2):
            load_dy(s, h).wait()
        pk[s] = dot(pmat[...], dyb[s]).astype(BF16).reshape(pk.shape[1:])

    def row_copy(s, spot, j):
        (sx, sy), (bx, by) = SPOTS[spot], TAKES[spot][j]
        e = (y + GY - by) % GY * GX + (x + GX - bx) % GX
        to = near((sx - bx) % GX, (sy - by) % GY, spot // 2)
        return pk.at[s, e], rx.at[s, spot % 2, c, j], pk_send.at[s, spot, j], rx_recv.at[s, spot % 2], to

    def send(copy, stays):
        src, dst, ss, rs, to = copy
        if stays is None:
            remote(src, dst, ss, rs, to).start()
        else:
            pl.when(stays)(lambda: pltpu.make_async_copy(src, dst, rs).start())
            pl.when(jnp.logical_not(stays))(lambda: remote(src, dst, ss, rs, to).start())

    def pieces(copy):
        src, dst, ss, rs, to = copy
        step = src.shape[0] // PIECES
        for n in range(PIECES):
            part = pl.ds(n * step, step)
            yield src.at[part], dst.at[part], ss.at[n], rs, to

    def sent(copy, stays):
        src, dst, ss, rs, to = copy
        if stays is None:
            remote(src, dst, ss, rs, to).wait_send()
        else:
            pl.when(jnp.logical_not(stays))(lambda: remote(src, dst, ss, rs, to).wait_send())

    def row_stays(spot, j):
        return c == spot // 2 if j == 0 else None

    def send_rows(s, e):
        for j in (1, 2, 3, 0):
            for spot in (e, e + 2):
                send(row_copy(s, spot, j), row_stays(spot, j))

    def reduced_copy(spot):
        to = near(*SPOTS[spot], spot // 2)
        return rl.at[spot], ra.at[spot % 2, c], r_send.at[spot], r_recv.at[spot % 2, c], to

    def reduced_stays(spot):
        return c == 0 if spot == 0 else None

    load_proj.wait()
    for e in range(2):
        for spot in (e, e + 2):
            for j in range(4):
                load_hid(spot, j).wait()
            rl[spot] = dot(hid[spot], proj[...]).astype(BF16).reshape(rl.shape[1:])
        if e == 0:
            pl.semaphore_wait(barrier, len(partners))
        for spot in (e, e + 2):
            for part in pieces(reduced_copy(spot)):
                send(part, reduced_stays(spot))
        if e == 0:
            pack(0)
        send_rows(0, e)

    @pl.loop(1, LEAD)
    def _(s):
        pack(s)
        for e in range(2):
            send_rows(s, e)

    def reduced_landed(e):
        for k in range(2):
            landed(ra.at[e, k], r_recv.at[e, k])
        got = ra[e].reshape(8 * CAP, ra.shape[-1])
        rt[e] = dot_nt(eye(got.shape[1]), got).astype(BF16)

    def partial(s, e):
        landed(rx.at[s, e], rx_recv.at[s, e])
        got = rx[s, e]
        total = dot(rt[e], got.reshape(8 * CAP, got.shape[-1]))
        half = total.shape[1] // 2
        return total[:, :half], total[:, half:]

    def z_copy(s, h, e, way, k):
        to = dev(x, y, (z + jnp.where(way == 0, 1, GZ - 1)) % GZ, c)
        return remote(
            zs.at[s, h, e], zr.at[way, k - 1, h, e], z_send.at[s, h, e], z_recv.at[way, k - 1, h, e], to
        )

    for e in range(2):
        reduced_landed(e)
        halves = partial(0, e)
        for h in range(2):
            zs[0, h, e] = halves[h].astype(BF16)
            z_copy(0, h, e, h, 4).start()
    pack(LEAD)
    for e in range(2):
        send_rows(LEAD, e)

    def pass_on(s):
        k = far(s)
        for e in range(2):
            halves = partial(s, e)
            for h in range(2):
                way = way_of(s, h)

                @pl.when(s != 1)
                def _():
                    landed(zr.at[way, k, h, e], z_recv.at[way, k, h, e])

                zs[s, h, e] = (halves[h] + zr[way, k, h, e].astype(F32)).astype(BF16)
                z_copy(s, h, e, way, k).start()

    @pl.loop(1, GZ - LEAD)
    def _(s):
        pass_on(s)
        pack(s + LEAD)
        for e in range(2):
            send_rows(s + LEAD, e)

    @pl.loop(GZ - LEAD, GZ - 1)
    def _(s):
        pass_on(s)

    def owner_copy(h, e):
        sx, sy = (jnp.where(c == 0, SPOTS[e][i], SPOTS[2 + e][i]) for i in range(2))
        to = near(GX - sx, GY - sy, h)
        return fs.at[h, e], fr.at[2 * c + e], f_send.at[h, e], f_recv.at[2 * c + e], to

    def owner_stays(h, e):
        return c == 0 if h == 0 and e == 0 else None

    for e in range(2):
        halves = partial(GZ - 1, e)
        for h in range(2):
            total = halves[h]
            for way in range(2):
                landed(zr.at[way, 0, h, e], z_recv.at[way, 0, h, e])
                total = total + zr[way, 0, h, e].astype(F32)
            fs[h, e] = total.astype(BF16)
            for part in pieces(owner_copy(h, e)):
                send(part, owner_stays(h, e))

    for spot in range(4):
        for part in pieces(reduced_copy(spot)):
            sent(part, reduced_stays(spot))

    @pl.loop(0, GZ)
    def _(s):
        for spot in range(4):
            for j in range(4):
                sent(row_copy(s, spot, j), row_stays(spot, j))

    @pl.loop(0, GZ - 1)
    def _(s):
        for h in range(2):
            for e in range(2):
                z_copy(s, h, e, 0, 1).wait_send()

    for k in range(4):
        landed(fr.at[k], f_recv.at[k])
    total = fr[0].astype(F32)
    for k in range(1, 4):
        total = total + fr[k].astype(F32)
    grad[...] = total.T

    for h in range(2):
        for e in range(2):
            for part in pieces(owner_copy(h, e)):
                sent(part, owner_stays(h, e))


def grads(dy, routes, gates, hidden, projector):
    tokens, width = dy.shape
    slots, features = hidden.shape
    rank = projector.shape[1]
    slab = width // GZ
    half = slab // 2
    dma = pltpu.SemaphoreType.DMA
    return pl.pallas_call(
        grad_kernel,
        out_shape=jax.ShapeDtypeStruct((half, rank), F32),
        in_specs=[
            pl.BlockSpec(memory_space=pl.ANY),
            pl.BlockSpec(memory_space=pltpu.VMEM),
            pl.BlockSpec(memory_space=pltpu.VMEM),
            pl.BlockSpec(memory_space=pl.ANY),
            pl.BlockSpec(memory_space=pl.ANY),
        ],
        out_specs=pl.BlockSpec(memory_space=pltpu.VMEM),
        scratch_shapes=[
            pltpu.VMEM((GZ, tokens, slab), BF16),
            pltpu.VMEM((4, 4 * CAP, features), BF16),
            pltpu.VMEM((features, rank), BF16),
            pltpu.VMEM((EXPERTS * CAP, tokens), BF16),
            pltpu.VMEM((GZ, EXPERTS, CAP, slab), BF16),
            pltpu.VMEM((4, 4, CAP, rank), BF16),
            pltpu.VMEM((2, 2, 4, CAP, rank), BF16),
            pltpu.VMEM((2, rank, 8 * CAP), BF16),
            pltpu.VMEM((GZ, 2, 2, 4, CAP, slab), BF16),
            pltpu.VMEM((GZ - 1, 2, 2, rank, half), BF16),
            pltpu.VMEM((2, 4, 2, 2, rank, half), BF16),
            pltpu.VMEM((2, 2, rank, half), BF16),
            pltpu.VMEM((4, rank, half), BF16),
            dma((5, 4)),
            dma((GZ, 2)),
            dma((4, PIECES)),
            dma((2, 2)),
            dma((GZ, 4, 4)),
            dma((GZ, 2)),
            dma((GZ - 1, 2, 2)),
            dma((2, 4, 2, 2)),
            dma((2, 2, PIECES)),
            dma((4,)),
        ],
        compiler_params=pltpu.CompilerParams(
            collective_id=0, has_side_effects=True, vmem_limit_bytes=58 * 2**20
        ),
        cost_estimate=pl.CostEstimate(flops=8 * 10**9, bytes_accessed=8 * 2**20, transcendentals=0),
    )(dy, routes, gates, hidden, projector)


def update_kernel(grad, one, two, projector, weights, new_weights, new_one, new_two):
    g = grad[...]
    first = beta_one * one[:, 0, :] + (1.0 - beta_one) * g
    second = beta_two * two[:, 0, :] + (1.0 - beta_two) * g * g
    new_one[:, 0, :] = first
    new_two[:, 0, :] = second
    direction = (first / (jnp.sqrt(second) + eps)).astype(BF16)
    for at in range(0, weights.shape[0], 256):
        rows = slice(at, at + 256)
        change = dot_nt(projector[rows, :], direction)
        new_weights[rows, :] = (weights[rows, :].astype(F32) - step_size * change).astype(BF16)


def update(grad, one, two, projector, weights):
    return pl.pallas_call(
        update_kernel,
        out_shape=(
            jax.ShapeDtypeStruct(weights.shape, BF16),
            jax.ShapeDtypeStruct(one.shape, F32),
            jax.ShapeDtypeStruct(two.shape, F32),
        ),
        compiler_params=pltpu.CompilerParams(vmem_limit_bytes=32 * 2**20),
    )(grad, one, two, projector, weights)


def body(dy_tokens, gates, routes, hidden, projector, weights, moment_one, moment_two):
    projector = projector[0]
    grad = grads(dy_tokens, routes.T, gates.T, hidden[0], projector)
    new_weights, new_one, new_two = update(grad, moment_one, moment_two, projector, weights[0])
    return (new_weights[None], new_one, new_two)


def solution(mesh):
    in_specs = (
        P(("dp", "expert"), None),
        P(("dp", "expert"), None),
        P(("dp", "expert"), None),
        P("expert", "dp", None),
        P("expert", None, None),
        P("expert", None, "dp"),
        P("dp", "expert", None),
        P("dp", "expert", None),
    )
    out_specs = (P("expert", None, "dp"), P("dp", "expert", None), P("dp", "expert", None))
    return jax.shard_map(body, mesh=mesh, in_specs=in_specs, out_specs=out_specs, check_vma=False)
```

```python
import jax
import jax.numpy as jnp
from jax import lax
from jax.experimental import pallas as pl
from jax.experimental.pallas import tpu as pltpu
from jax.sharding import PartitionSpec as P

EXPERTS = 16
CAP = 64
GX, GY, GZ = 4, 4, 8
LEAD = 2
PIECES = 2
MESH = pl.DeviceIdType.MESH

beta_one = 0.9
beta_two = 0.999
eps = 1e-06
step_size = 0.02

F32, BF16 = jnp.float32, jnp.bfloat16


def dot(a, b):
    return jnp.dot(a, b, preferred_element_type=F32)


def dot_nt(a, b):
    return lax.dot_general(a, b, (((1,), (1,)), ((), ())), preferred_element_type=F32)


def eye(n):
    same = lax.broadcasted_iota(jnp.int32, (n, n), 0) == lax.broadcasted_iota(jnp.int32, (n, n), 1)
    return jnp.where(same, 1.0, 0.0).astype(BF16)


SPOTS = ((0, 0), (1, 1), (3, 2), (2, 3))
TAKES = (
    ((0, 0), (0, 1), (0, 3), (3, 0)),
    ((1, 1), (1, 0), (1, 2), (2, 1)),
    ((3, 2), (0, 2), (2, 2), (3, 1)),
    ((2, 3), (1, 3), (2, 0), (3, 3)),
)


def grad_kernel(
    dy, routes, gates, hidden, projector, grad,
    dyb, hid, proj, pmat, pk, rl, ra, rt, rx, zs, zr, fs, fr,
    load_sem, dy_sem, r_send, r_recv, pk_send, rx_recv, z_send, z_recv, f_send, f_recv,
):
    dp, ex = lax.axis_index("dp"), lax.axis_index("expert")
    x, y, z, c = ex % GX, ex // GX, dp // 2, dp % 2

    def dev(x, y, z, c):
        return (z * 2 + c, y * GX + x)

    def near(dx, dy, c):
        return dev((x + dx) % GX, (y + dy) % GY, z, c)

    def remote(src, dst, send, recv, to):
        return pltpu.make_async_remote_copy(src, dst, send, recv, device_id=to, device_id_type=MESH)

    def landed(buf, sem):
        pltpu.make_async_copy(buf, buf, sem).wait()

    def far(s):
        return (8 - s) // 2

    def way_of(s, h):
        return (s + h) % 2

    def load_dy(s, h):
        half = dyb.shape[2] // 2
        slab = (z + jnp.where(way_of(s, h) == 0, far(s), GZ - far(s))) % GZ
        at = pl.multiple_of((slab * 2 + h) * half, half)
        return pltpu.make_async_copy(
            dy.at[:, pl.ds(at, half)], dyb.at[s, :, pl.ds(h * half, half)], dy_sem.at[s, h]
        )

    def load_hid(spot, j):
        dx, ddy = TAKES[spot][j]
        block = (y + ddy) % GY * GX + (x + dx) % GX
        return pltpu.make_async_copy(
            hidden.at[pl.ds(pl.multiple_of(block * CAP, CAP), CAP)], hid.at[spot, pl.ds(j * CAP, CAP)], load_sem.at[spot, j]
        )

    load_proj = pltpu.make_async_copy(projector, proj, load_sem.at[4, 0])
    for h in range(2):
        load_dy(0, h).start()
    load_proj.start()
    for spot in (0, 2, 1, 3):
        for j in range(4):
            load_hid(spot, j).start()

    @pl.loop(1, GZ)
    def _(s):
        for h in range(2):
            load_dy(s, h).start()

    barrier = pltpu.get_barrier_semaphore()
    steps = [(1, 0), (3, 0), (0, 1), (0, 3)]
    for dx, ddy in SPOTS[1:]:
        steps += [(dx, ddy), ((GX - dx) % GX, (GY - ddy) % GY)]
    partners = [near(dx, ddy, core) for dx, ddy in steps for core in range(2)] + [dev(x, y, z, 1 - c)]
    partners += [dev(x, y, (z + 1) % GZ, c), dev(x, y, (z + GZ - 1) % GZ, c)]
    for to in partners:
        pl.semaphore_signal(barrier, inc=1, device_id=to, device_id_type=MESH)

    zr[0, 3, 1] = jnp.zeros(zr.shape[3:], BF16)
    zr[1, 3, 0] = jnp.zeros(zr.shape[3:], BF16)

    tokens = routes.shape[1]
    ids = routes[...]
    here = ids < EXPERTS
    expert = jnp.sum(jnp.where(here, ids, 0), axis=0, keepdims=True)
    gate = jnp.sum(jnp.where(here, gates[...].astype(F32), 0.0), axis=0, keepdims=True)
    chosen = lax.broadcasted_iota(jnp.int32, (EXPERTS, tokens), 0) == expert
    earlier = lax.broadcasted_iota(jnp.int32, (tokens, tokens), 0) < lax.broadcasted_iota(
        jnp.int32, (tokens, tokens), 1
    )
    count = dot(jnp.where(chosen, 1.0, 0.0).astype(BF16), jnp.where(earlier, 1.0, 0.0).astype(BF16))
    rank = jnp.sum(jnp.where(chosen, count, 0.0), axis=0, keepdims=True).astype(jnp.int32)
    slot = expert * CAP + rank
    for e in range(0, EXPERTS, 4):
        at = lax.broadcasted_iota(jnp.int32, (4 * CAP, tokens), 0) + e * CAP
        pmat[e * CAP : (e + 4) * CAP, :] = jnp.where(at == slot, gate, 0.0).astype(BF16)

    def pack(s):
        for h in range(2):
            load_dy(s, h).wait()
        pk[s] = dot(pmat[...], dyb[s]).astype(BF16).reshape(pk.shape[1:])

    def row_copy(s, spot, j):
        (sx, sy), (bx, by) = SPOTS[spot], TAKES[spot][j]
        e = (y + GY - by) % GY * GX + (x + GX - bx) % GX
        to = near((sx - bx) % GX, (sy - by) % GY, spot // 2)
        return pk.at[s, e], rx.at[s, spot % 2, c, j], pk_send.at[s, spot, j], rx_recv.at[s, spot % 2], to

    def send(copy, stays):
        src, dst, ss, rs, to = copy
        if stays is None:
            remote(src, dst, ss, rs, to).start()
        else:
            pl.when(stays)(lambda: pltpu.make_async_copy(src, dst, rs).start())
            pl.when(jnp.logical_not(stays))(lambda: remote(src, dst, ss, rs, to).start())

    def pieces(copy):
        src, dst, ss, rs, to = copy
        step = src.shape[0] // PIECES
        for n in range(PIECES):
            part = pl.ds(n * step, step)
            yield src.at[part], dst.at[part], ss.at[n], rs, to

    def sent(copy, stays):
        src, dst, ss, rs, to = copy
        if stays is None:
            remote(src, dst, ss, rs, to).wait_send()
        else:
            pl.when(jnp.logical_not(stays))(lambda: remote(src, dst, ss, rs, to).wait_send())

    def row_stays(spot, j):
        return c == spot // 2 if j == 0 else None

    def send_rows(s, e):
        for j in (1, 2, 3, 0):
            for spot in (e, e + 2):
                send(row_copy(s, spot, j), row_stays(spot, j))

    def reduced_copy(spot):
        to = near(*SPOTS[spot], spot // 2)
        return rl.at[spot], ra.at[spot % 2, c], r_send.at[spot], r_recv.at[spot % 2, c], to

    def reduced_stays(spot):
        return c == 0 if spot == 0 else None

    load_proj.wait()
    for e in range(2):
        for spot in (e, e + 2):
            for j in range(4):
                load_hid(spot, j).wait()
            rl[spot] = dot(hid[spot], proj[...]).astype(BF16).reshape(rl.shape[1:])
        if e == 0:
            pl.semaphore_wait(barrier, len(partners))
        for spot in (e, e + 2):
            for part in pieces(reduced_copy(spot)):
                send(part, reduced_stays(spot))
        if e == 0:
            pack(0)
        send_rows(0, e)

    @pl.loop(1, LEAD)
    def _(s):
        pack(s)
        for e in (1, 0):
            send_rows(s, e)

    def reduced_landed(e):
        for k in range(2):
            landed(ra.at[e, k], r_recv.at[e, k])
        got = ra[e].reshape(8 * CAP, ra.shape[-1])
        rt[e] = dot_nt(eye(got.shape[1]), got).astype(BF16)

    def partial(s, e):
        landed(rx.at[s, e], rx_recv.at[s, e])
        got = rx[s, e]
        total = dot(rt[e], got.reshape(8 * CAP, got.shape[-1]))
        half = total.shape[1] // 2
        return total[:, :half], total[:, half:]

    def z_copy(s, h, e, way, k):
        to = dev(x, y, (z + jnp.where(way == 0, 1, GZ - 1)) % GZ, c)
        return remote(
            zs.at[s, h, e], zr.at[way, k - 1, h, e], z_send.at[s, h, e], z_recv.at[way, k - 1, h, e], to
        )

    for e in range(2):
        reduced_landed(e)
        halves = partial(0, e)
        for h in range(2):
            zs[0, h, e] = halves[h].astype(BF16)
            z_copy(0, h, e, h, 4).start()
    pack(LEAD)
    for e in (1, 0):
        send_rows(LEAD, e)

    def pass_on(s):
        k = far(s)
        for e in (1, 0):
            halves = partial(s, e)
            for h in range(2):
                way = way_of(s, h)

                @pl.when(s != 1)
                def _():
                    landed(zr.at[way, k, h, e], z_recv.at[way, k, h, e])

                zs[s, h, e] = (halves[h] + zr[way, k, h, e].astype(F32)).astype(BF16)
                z_copy(s, h, e, way, k).start()

    @pl.loop(1, GZ - LEAD)
    def _(s):
        pass_on(s)
        pack(s + LEAD)
        for e in (1, 0):
            send_rows(s + LEAD, e)

    @pl.loop(GZ - LEAD, GZ - 1)
    def _(s):
        pass_on(s)

    def owner_copy(h, e):
        sx, sy = (jnp.where(c == 0, SPOTS[e][i], SPOTS[2 + e][i]) for i in range(2))
        to = near(GX - sx, GY - sy, h)
        return fs.at[h, e], fr.at[2 * c + e], f_send.at[h, e], f_recv.at[2 * c + e], to

    def owner_stays(h, e):
        return c == 0 if h == 0 and e == 0 else None

    for e in (1, 0):
        halves = partial(GZ - 1, e)
        for h in range(2):
            total = halves[h]
            for way in range(2):
                landed(zr.at[way, 0, h, e], z_recv.at[way, 0, h, e])
                total = total + zr[way, 0, h, e].astype(F32)
            fs[h, e] = total.astype(BF16)
            for part in pieces(owner_copy(h, e)):
                send(part, owner_stays(h, e))

    for spot in range(4):
        for part in pieces(reduced_copy(spot)):
            sent(part, reduced_stays(spot))

    @pl.loop(0, GZ)
    def _(s):
        for spot in range(4):
            for j in range(4):
                sent(row_copy(s, spot, j), row_stays(spot, j))

    @pl.loop(0, GZ - 1)
    def _(s):
        for h in range(2):
            for e in range(2):
                z_copy(s, h, e, 0, 1).wait_send()

    for k in range(4):
        landed(fr.at[k], f_recv.at[k])
    total = fr[0].astype(F32)
    for k in range(1, 4):
        total = total + fr[k].astype(F32)
    grad[...] = total.T

    for h in range(2):
        for e in range(2):
            for part in pieces(owner_copy(h, e)):
                sent(part, owner_stays(h, e))


def grads(dy, routes, gates, hidden, projector):
    tokens, width = dy.shape
    slots, features = hidden.shape
    rank = projector.shape[1]
    slab = width // GZ
    half = slab // 2
    dma = pltpu.SemaphoreType.DMA
    return pl.pallas_call(
        grad_kernel,
        out_shape=jax.ShapeDtypeStruct((half, rank), F32),
        in_specs=[
            pl.BlockSpec(memory_space=pl.ANY),
            pl.BlockSpec(memory_space=pltpu.VMEM),
            pl.BlockSpec(memory_space=pltpu.VMEM),
            pl.BlockSpec(memory_space=pl.ANY),
            pl.BlockSpec(memory_space=pl.ANY),
        ],
        out_specs=pl.BlockSpec(memory_space=pltpu.VMEM),
        scratch_shapes=[
            pltpu.VMEM((GZ, tokens, slab), BF16),
            pltpu.VMEM((4, 4 * CAP, features), BF16),
            pltpu.VMEM((features, rank), BF16),
            pltpu.VMEM((EXPERTS * CAP, tokens), BF16),
            pltpu.VMEM((GZ, EXPERTS, CAP, slab), BF16),
            pltpu.VMEM((4, 4, CAP, rank), BF16),
            pltpu.VMEM((2, 2, 4, CAP, rank), BF16),
            pltpu.VMEM((2, rank, 8 * CAP), BF16),
            pltpu.VMEM((GZ, 2, 2, 4, CAP, slab), BF16),
            pltpu.VMEM((GZ - 1, 2, 2, rank, half), BF16),
            pltpu.VMEM((2, 4, 2, 2, rank, half), BF16),
            pltpu.VMEM((2, 2, rank, half), BF16),
            pltpu.VMEM((4, rank, half), BF16),
            dma((5, 4)),
            dma((GZ, 2)),
            dma((4, PIECES)),
            dma((2, 2)),
            dma((GZ, 4, 4)),
            dma((GZ, 2)),
            dma((GZ - 1, 2, 2)),
            dma((2, 4, 2, 2)),
            dma((2, 2, PIECES)),
            dma((4,)),
        ],
        compiler_params=pltpu.CompilerParams(
            collective_id=0, has_side_effects=True, vmem_limit_bytes=58 * 2**20
        ),
        cost_estimate=pl.CostEstimate(flops=8 * 10**9, bytes_accessed=8 * 2**20, transcendentals=0),
    )(dy, routes, gates, hidden, projector)


def update_kernel(grad, one, two, projector, weights, new_weights, new_one, new_two):
    g = grad[...]
    first = beta_one * one[:, 0, :] + (1.0 - beta_one) * g
    second = beta_two * two[:, 0, :] + (1.0 - beta_two) * g * g
    new_one[:, 0, :] = first
    new_two[:, 0, :] = second
    direction = (first / (jnp.sqrt(second) + eps)).astype(BF16)
    for at in range(0, weights.shape[0], 256):
        rows = slice(at, at + 256)
        change = dot_nt(projector[rows, :], direction)
        new_weights[rows, :] = (weights[rows, :].astype(F32) - step_size * change).astype(BF16)


def update(grad, one, two, projector, weights):
    return pl.pallas_call(
        update_kernel,
        out_shape=(
            jax.ShapeDtypeStruct(weights.shape, BF16),
            jax.ShapeDtypeStruct(one.shape, F32),
            jax.ShapeDtypeStruct(two.shape, F32),
        ),
        compiler_params=pltpu.CompilerParams(vmem_limit_bytes=32 * 2**20),
    )(grad, one, two, projector, weights)


def body(dy_tokens, gates, routes, hidden, projector, weights, moment_one, moment_two):
    projector = projector[0]
    grad = grads(dy_tokens, routes.T, gates.T, hidden[0], projector)
    new_weights, new_one, new_two = update(grad, moment_one, moment_two, projector, weights[0])
    return (new_weights[None], new_one, new_two)


def solution(mesh):
    in_specs = (
        P(("dp", "expert"), None),
        P(("dp", "expert"), None),
        P(("dp", "expert"), None),
        P("expert", "dp", None),
        P("expert", None, None),
        P("expert", None, "dp"),
        P("dp", "expert", None),
        P("dp", "expert", None),
    )
    out_specs = (P("expert", None, "dp"), P("dp", "expert", None), P("dp", "expert", None))
    return jax.shard_map(body, mesh=mesh, in_specs=in_specs, out_specs=out_specs, check_vma=False)
```
